32 devices in a mesh: groups: 2 (over x), req: 16 (over z, y, core).
Axes of the slice: x: 2, y: 2, z: 4, core: 2. Of those that a mesh axis runs over, the one named last changes fastest.
Arguments:
- frames: bfloat16 [8192, 1280], P(('groups', 'req')), parts along dimension 0, may hold values from -6 to 6
- ln1_gain: bfloat16 [1280], replicated, may hold values from 0.5 to 1.5
- ln1_bias: bfloat16 [1280], replicated, may hold values from -3 to 3
- w_qkv: bfloat16 [2560, 3840], P('req'), may hold values from -1 to 1
- w_out: bfloat16 [2560, 1280], P('req'), may hold values from -0.15625 to 0.15625
- ln2_gain: bfloat16 [1280], replicated, may hold values from 0.5 to 1.5
- ln2_bias: bfloat16 [1280], replicated, may hold values from -3 to 3
- w_proj: bfloat16 [2560, 4096], P('req'), may hold values from -1 to 1, as said below
- b_proj: bfloat16 [4096], replicated, may hold values from -3 to 3
- text_embed: bfloat16 [8192, 4096], P(('groups', 'req')), parts along dimension 0, may hold values from -6 to 6
- rms_gain: bfloat16 [4096], replicated, may hold values from 0.5 to 1.5
- window_pairs: int32 [32, 4], P(('groups', 'req')), parts along dimension 0, may hold values from 1 to 64, 128 in all within a row
- row_route: int32 [4096, 1], P('groups'), parts along dimension 0, may hold values from 0 to 15; in each aligned block of 128 rows (0 to 127, 128 to 255, ...) at most 16 rows name the same one
Outputs:
- prefill_input: bfloat16 [16384, 4096], P(('groups', 'req')), parts along dimension 0
The draws below stay inside these ranges and needn't reach their ends.
There are 2 independent parts, one for each index of `groups`. The reference program is written for one: setup_inputs(seed, part) draws one part's arguments, and reference() takes and returns one part's arrays. A program takes and returns all parts, laid end to end along the dimension named above; an argument that names none is the same for every part. Nothing has to cross between parts.
Inputs may be any that keep to these rules, and one draw needn't show every extreme that they name: `w_proj`: its 2 blocks of 1280 rows are equal. `window_pairs`: row j of device s gives the frame pairs of the j-th window of its queue; each row sums to 128. `row_route`: the pooled rows of one device name each prefill device at most 16 times.
All inputs are finite; a program needn't handle non-finite values.
Results may differ from the reference program's by a relative error of at most 0.0047.
Values may be sent and summed in bfloat16 or wider, within the bound.
A program may use at most 128 MiB of HBM per device.

```python
import math
import jax
import jax.numpy as jnp
import numpy as np
from jax import lax

EW = 1280
LW = 4096
HEAD = 64
TGROUP = 8
EH = 20
COPIES = 2
ROWS = 256
TEXT = 256
WPAIR = 64
POOLED = 128
WPD = 4
CAP = 16
STRETCH = 512
N_REQ = 16


def draw_w_qkv(key, part):
    key = jax.random.fold_in(key, 11)
    query_key, second_key, value_key = jax.random.split(key, 3)
    weight_scale = EW ** (-0.5)
    query_part = jax.random.normal(query_key, (COPIES, EW, EW), jnp.float32) * weight_scale
    value_part = jax.random.normal(value_key, (COPIES, EW, EW), jnp.float32) * weight_scale
    key_part = jax.random.normal(second_key, (COPIES, EW, EW), jnp.float32) * weight_scale
    stacked = jnp.concatenate([query_part, key_part, value_part], axis=2)
    return jnp.clip(stacked, -1.0, 1.0).reshape(COPIES * EW, 3 * EW).astype(jnp.bfloat16)


def draw_w_proj(key, part):
    key = jax.random.fold_in(key, 13)
    single = jax.random.normal(key, (EW, LW), jnp.float32) * EW ** (-0.5)
    single = jnp.clip(single, -1.0, 1.0)
    return jnp.tile(single, (COPIES, 1)).astype(jnp.bfloat16)


def block_levels(own_key, dims, pieces, low, high):
    level, own = 1.0, jax.random.fold_in(own_key, 6)
    for position, shards_of in pieces:
        steps = jnp.exp(jax.random.uniform(jax.random.fold_in(own, position), (shards_of,), jnp.float32, low / len(pieces), high / len(pieces)))
        level = level * jnp.repeat(steps, dims[position] // shards_of).reshape([-1 if axis == position else 1 for axis in range(len(dims))])
    return level


def length_profile(count, total, limit, skew):
    weights = [(1 << 20) // math.isqrt(standing ** skew) + 1 for standing in range(2, count + 1)]
    spare, given = total - limit - (count - 1), [1] * (count - 1)
    while spare > 0:
        movable = [i for i in range(count - 1) if given[i] < limit]
        whole, left = sum([weights[i] for i in movable]), spare
        for i in movable:
            more = min(limit - given[i], max(1, left * weights[i] // whole), spare)
            given[i] = given[i] + more
            spare = spare - more
    return np.array([limit] + given)


def ragged(stream_key, amount, total, most, slope):
    if amount == 2:
        one = jax.random.randint(stream_key, (), max(1, total - most), min(most, total - 1) + 1)
        return jnp.stack([one, total - one])
    tallies = jnp.asarray(length_profile(amount, total, most, slope), jnp.int32)
    couples = (amount - 1) // 2
    donor, receiver = tallies[1:1 + 2 * couples:2], tallies[2:2 + 2 * couples:2]
    margin = jnp.minimum(donor - 1, most - receiver)
    passed = jax.random.randint(jax.random.fold_in(stream_key, 1), (couples,), 0, 1 << 20) % (margin + 1)
    tallies = tallies.at[1:1 + 2 * couples:2].set(donor - passed).at[2:2 + 2 * couples:2].set(receiver + passed)
    return tallies[jax.random.permutation(jax.random.fold_in(stream_key, 2), amount)]


def deal_out(key, own, number, rows, amount, top, limit, skew):
    sequence = jax.random.permutation(key, amount)
    heavy_load, common = load_shares(amount, rows * top, limit, skew, True), load_shares(amount, rows * top, limit, skew, False)
    places = jnp.arange(amount)

    def named(tallies, offset_by):
        used = int((tallies > 0).sum())
        fixed = max(1, used // 4)
        passed = fixed + (places - fixed + offset_by * (used - fixed)) % max(1, amount - fixed)
        return jnp.zeros((amount,), jnp.int32).at[sequence[jnp.where(places < fixed, places, passed)]].set(jnp.asarray(tallies, jnp.int32))

    tallies = jnp.where(number % 4 == 0, named(heavy_load, number // 4), named(common, number - number // 4 - 1))
    mixed = jax.random.permutation(jax.random.fold_in(own, 3), amount)
    donor, receiver = mixed[0:amount // 2 * 2:2], mixed[1:amount // 2 * 2:2]
    slack = jnp.minimum(tallies[donor] - 1, limit - tallies[receiver]) // 2
    slack = jnp.where((donor == sequence[0]) | (receiver == sequence[0]) | (tallies[receiver] == 0), 0, jnp.maximum(slack, 0))
    passed = jax.random.randint(jax.random.fold_in(own, 4), (amount // 2,), 0, 1 << 20) % (slack + 1)
    tallies = tallies.at[donor].add(-passed).at[receiver].add(passed)
    items = jnp.searchsorted(jnp.cumsum(tallies), jnp.arange(rows * top), side="right").astype(jnp.int32)
    table = items.reshape(top, rows).T
    table = table[jax.random.permutation(jax.random.fold_in(own, 1), rows)]
    offset_by = jax.random.randint(jax.random.fold_in(own, 2), (rows, 1), 0, top)
    return jnp.take_along_axis(table, (jnp.arange(top)[None, :] + offset_by) % top, axis=1)


def load_shares(count, total, reach, slope, full):
    weights = [(1 << 20) // math.isqrt(standing ** slope) + 1 for standing in range(1, count + 1)]
    largest = reach if full else min(reach, max(-(-total // count), total * weights[0] // sum(weights)))
    least = 1 if total - largest >= count - 1 else 0
    holding, spare = [largest] + [least] * (count - 1), total - largest - least * (count - 1)
    while spare > 0:
        movable = [i for i in range(1, count) if holding[i] < largest] or [i for i in range(1, count) if holding[i] < reach]
        whole, left = sum([weights[i] for i in movable]), spare
        for i in movable:
            addition = min(reach - holding[i], max(1, left * weights[i] // whole), spare)
            holding[i] = holding[i] + addition
            spare = spare - addition
    return np.array(holding)


def noise(key, dims, spread, bound, shards=(), kind=jnp.bfloat16):
    entries = jax.random.normal(key, dims, jnp.float32) * spread
    if len(shards) > 0:
        entries = block_levels(key, dims, shards, -0.22, 0.18) * entries
    return jnp.clip(entries, min=-bound, max=bound).astype(kind)


def setup_inputs(seed: int = 0, part: int = 0) -> dict:
    streams_of = jax.random.split(jax.random.key(seed), 14)
    part_keys = jax.random.split(jax.random.fold_in(streams_of[13], part), 14)
    frames = noise(part_keys[0], (N_REQ * ROWS, EW), 1.0, 6.0, ((0, 16),))
    ln1_gain = jnp.clip(1.0 + 0.1 * jax.random.normal(streams_of[1], (EW,), jnp.float32), 0.5, 1.5).astype(jnp.bfloat16)
    ln1_bias = noise(streams_of[2], (EW,), 0.5, 3.0)
    w_qkv = draw_w_qkv(jax.random.fold_in(streams_of[13], 71), part)
    w_out = noise(streams_of[4], (COPIES * EW, EW), EW ** -0.5, 0.15625, ((0, 16),))
    ln2_gain = jnp.clip(1.0 + 0.1 * jax.random.normal(streams_of[5], (EW,), jnp.float32), 0.5, 1.5).astype(jnp.bfloat16)
    ln2_bias = noise(streams_of[6], (EW,), 0.5, 3.0)
    w_proj = draw_w_proj(jax.random.fold_in(streams_of[13], 71), part)
    b_proj = noise(streams_of[8], (LW,), 0.5, 3.0)
    text_embed = noise(part_keys[9], (N_REQ * TEXT, LW), 1.0, 6.0, ((0, 16),))
    rms_gain = jnp.clip(1.0 + 0.1 * jax.random.normal(streams_of[10], (LW,), jnp.float32), 0.5, 1.5).astype(jnp.bfloat16)
    window_pairs = jax.vmap(lambda own: ragged(own, WPD, POOLED, WPAIR, 2))(jax.random.split(part_keys[11], N_REQ)).reshape((N_REQ, WPD)).astype(jnp.int32)
    row_route_keys = jax.random.split(jax.random.fold_in(part_keys[12], 1), (N_REQ * POOLED) // POOLED)
    row_route_turns = jax.random.permutation(jax.random.fold_in(part_keys[12], 3), (N_REQ * POOLED) // POOLED)
    row_route = jax.vmap(lambda own, number: deal_out(jax.random.fold_in(part_keys[12], 2), own, number, POOLED, N_REQ, 1, CAP, 2))(row_route_keys, row_route_turns).reshape((N_REQ * POOLED, 1))
    return {"frames": frames, "ln1_gain": ln1_gain, "ln1_bias": ln1_bias, "w_qkv": w_qkv, "w_out": w_out, "ln2_gain": ln2_gain, "ln2_bias": ln2_bias, "w_proj": w_proj, "b_proj": b_proj, "text_embed": text_embed, "rms_gain": rms_gain, "window_pairs": window_pairs, "row_route": row_route}


def layer_norm(values_in, gain_row, bias_row, epsilon):
    row_mean = lax.optimization_barrier(jnp.mean(values_in, axis=-1, keepdims=True))
    centered = values_in - row_mean
    variance = lax.optimization_barrier(jnp.mean(centered * centered, axis=-1, keepdims=True))
    return centered * lax.rsqrt(variance + epsilon) * gain_row.astype(jnp.float32) + bias_row.astype(jnp.float32)

def window_ids(pair_counts, frame_count):
    window_ends = jnp.cumsum(pair_counts.astype(jnp.int32)) * 2
    frame_index = jnp.arange(frame_count, dtype=jnp.int32)
    return lax.optimization_barrier(jnp.sum((frame_index[:, None] >= window_ends[None, :]).astype(jnp.int32), axis=1))

def encode(frames, pair_counts, ln1_gain, ln1_bias, w_qkv, w_out, ln2_gain, ln2_bias):
    frame_count = frames.shape[0]
    frames_f32 = frames.astype(jnp.float32)
    normed_in = layer_norm(frames_f32, ln1_gain, ln1_bias, 1e-05).astype(jnp.bfloat16)
    qkv_proj = jnp.dot(normed_in, w_qkv, preferred_element_type=jnp.float32)
    queries = qkv_proj[:, :EW].astype(jnp.bfloat16).reshape(frame_count, EH, HEAD)
    key_rows = qkv_proj[:, EW:2 * EW].astype(jnp.bfloat16).reshape(frame_count, EH, HEAD)
    value_rows = qkv_proj[:, 2 * EW:].astype(jnp.bfloat16).reshape(frame_count, EH, HEAD)
    window = window_ids(pair_counts, frame_count)
    same_window = window[:, None] == window[None, :]
    scores = jnp.einsum('qhd,khd->hqk', queries.astype(jnp.float32), key_rows.astype(jnp.float32)) * HEAD ** (-0.5)
    scores = jnp.where(same_window[None], scores, -1e+30)
    top_score = lax.optimization_barrier(jnp.max(scores, axis=2, keepdims=True))
    expo_scores = jnp.exp(scores - top_score)
    weights = (expo_scores / lax.optimization_barrier(jnp.sum(expo_scores, axis=2, keepdims=True))).astype(jnp.bfloat16)
    attended = jnp.einsum('hqk,khd->qhd', weights.astype(jnp.float32), value_rows.astype(jnp.float32))
    attended = attended.astype(jnp.bfloat16).reshape(frame_count, EW)
    encoded = frames_f32 + jnp.dot(attended, w_out, preferred_element_type=jnp.float32)
    pooled = (encoded[0::2] + encoded[1::2]) * 0.5
    return layer_norm(pooled, ln2_gain, ln2_bias, 1e-05).astype(jnp.bfloat16)

def rms_rows(packed_rows, rms_gain):
    values_f32 = packed_rows.astype(jnp.float32)
    mean_square = lax.optimization_barrier(jnp.mean(values_f32 * values_f32, axis=-1, keepdims=True))
    return (values_f32 * lax.rsqrt(mean_square + 1e-06) * rms_gain.astype(jnp.float32)).astype(jnp.bfloat16)

def reference(frames, ln1_gain, ln1_bias, w_qkv, w_out, ln2_gain, ln2_bias, w_proj, b_proj, text_embed, rms_gain, window_pairs, row_route):
    frame_blocks = frames.reshape(COPIES, TGROUP, ROWS, EW)
    pair_blocks = window_pairs.reshape(COPIES, TGROUP, WPD)
    qkv_copies = w_qkv.reshape(COPIES, EW, 3 * EW)
    out_copies = w_out.reshape(COPIES, EW, EW)
    proj_copies = w_proj.reshape(COPIES, EW, LW)

    def group_work(group_args):
        group_frames, group_pairs, qkv_copy, out_copy, proj_copy = group_args

        def encode_one(device_args):
            return encode(device_args[0], device_args[1], ln1_gain, ln1_bias, qkv_copy, out_copy, ln2_gain, ln2_bias)
        normed = lax.map(encode_one, (group_frames, group_pairs)).reshape(TGROUP * POOLED, EW)
        projected = jnp.dot(normed, proj_copy, preferred_element_type=jnp.float32) + b_proj.astype(jnp.float32)
        return projected.astype(jnp.bfloat16)
    audio_embed = lax.map(group_work, (frame_blocks, pair_blocks, qkv_copies, out_copies, proj_copies)).reshape(N_REQ * POOLED, LW)
    dest_rows = row_route[:, 0].astype(jnp.int32)
    one_hot = (dest_rows.reshape(N_REQ, POOLED)[:, :, None] == jnp.arange(N_REQ, dtype=jnp.int32)[None, None, :]).astype(jnp.int32)
    earlier = jnp.cumsum(one_hot, axis=1) - one_hot
    slot_index = lax.optimization_barrier(jnp.sum(earlier * one_hot, axis=2)).reshape(-1).astype(jnp.int32)
    source_dev = jnp.repeat(jnp.arange(N_REQ, dtype=jnp.int32), POOLED)
    audio_place = dest_rows * STRETCH + source_dev * CAP + slot_index
    packed = jnp.zeros((N_REQ * STRETCH, LW), jnp.bfloat16).at[audio_place].set(audio_embed)
    text_place = (jnp.arange(N_REQ, dtype=jnp.int32)[:, None] * STRETCH + 2 * POOLED + jnp.arange(TEXT, dtype=jnp.int32)[None, :]).reshape(-1)
    packed = packed.at[text_place].set(text_embed)
    normed_out = lax.map(lambda packed_rows: rms_rows(packed_rows, rms_gain), packed.reshape(N_REQ, STRETCH, LW))
    return normed_out.reshape(N_REQ * STRETCH, LW)
```

```python
import jax
import jax.numpy as jnp
from jax import lax
from jax.experimental import pallas as pl
from jax.experimental.pallas import tpu as pltpu
from jax.sharding import PartitionSpec as P

HEAD = 64
GROUP = 8
MESH = pl.DeviceIdType.MESH
F32 = jnp.float32
BF16 = jnp.bfloat16


def flipped(index, bit):
    return index + bit - 2 * bit * ((index // bit) % 2)


def norm_rows(values, gain, bias):
    mean = jnp.mean(values, axis=-1, keepdims=True)
    centered = values - mean
    variance = jnp.mean(centered * centered, axis=-1, keepdims=True)
    return centered * lax.rsqrt(variance + 1e-05) * gain + bias


def encoder_kernel(
    frames_ref, gain1_ref, bias1_ref, gain2_ref, bias2_ref, pairs_ref,
    qkv_ref, out_w_ref, proj_ref,
    normed_ref, whole_proj,
    whole_qkv, whole_out, normed_in, residual, qkv, attended, mask,
    send_sem, recv_sem, local_sem,
):
    width = frames_ref.shape[1]
    rows = frames_ref.shape[0]
    half = rows // 2
    shard = qkv_ref.shape[0]
    g = lax.axis_index("groups")
    r = lax.axis_index("req")
    lane = g % 2
    mine = r % GROUP
    core_dev = (g, flipped(r, 1))
    y_dev = (g, flipped(r, 2))
    z_dev = (g, flipped(r, 4))
    x_dev = (flipped(g, 1), r)
    own = mine
    from_y = flipped(mine, 2)
    from_z = flipped(mine, 4)
    from_yz = flipped(from_y, 4)

    barrier = pltpu.get_barrier_semaphore()
    for device in (core_dev, y_dev, z_dev, x_dev):
        pl.semaphore_signal(barrier, inc=1, device_id=device, device_id_type=MESH)
    pl.semaphore_wait(barrier, 4)

    pieces = 4
    proj_cols = proj_ref.shape[1] // pieces
    units = [(qkv_ref, whole_qkv, j * width, width) for j in range(3)]
    units.append((out_w_ref, whole_out, 0, width))
    units += [(proj_ref, whole_proj, j * proj_cols, proj_cols) for j in range(pieces)]
    count = len(units)
    tile = 16
    step = shard // (5 * tile) * tile
    direct = shard - step
    middle = shard // 2
    first = middle // tile // 2 * tile
    second = middle - first

    def view(unit, block, start, size):
        _, whole, column, columns = units[unit]
        begin = pl.multiple_of(block * shard + start, tile)
        return whole.at[pl.ds(begin, size), pl.ds(column, columns)]

    def own_view(unit, start, size):
        source, _, column, columns = units[unit]
        return source.at[pl.ds(pl.multiple_of(start, tile), size), pl.ds(column, columns)]

    def remote(unit, which, source, target, device):
        return pltpu.make_async_remote_copy(
            src_ref=source,
            dst_ref=target,
            send_sem=send_sem.at[unit, which],
            recv_sem=recv_sem.at[unit, which],
            device_id=device,
            device_id_type=MESH,
        )

    def moved(unit, which, block, start, size, device):
        span = view(unit, block, start, size)
        return remote(unit, which, span, span, device)

    def split(unit):
        return (second, first) if unit % 2 else (first, second)

    copies = []
    locals_ = []
    for u in range(count):
        via_y, via_z = split(u)
        d0 = lane * step
        m0 = lane * middle
        copies.append([
            remote(u, 0, own_view(u, d0, direct), view(u, own, d0, direct), y_dev),
            remote(u, 1, own_view(u, d0, direct), view(u, own, d0, direct), z_dev),
            remote(u, 2, own_view(u, 0, shard), view(u, own, 0, shard), core_dev),
            moved(u, 3, from_y, lane * direct, step, x_dev),
            moved(u, 4, from_y, m0 + via_y, via_z, z_dev),
            moved(u, 5, from_y, 0, shard, core_dev),
            moved(u, 6, from_z, lane * direct, step, x_dev),
            moved(u, 7, from_z, m0, via_y, y_dev),
            moved(u, 8, from_z, 0, shard, core_dev),
            moved(u, 9, from_yz, m0 + via_y, via_z, x_dev),
            moved(u, 10, from_yz, m0, via_y, x_dev),
            moved(u, 11, from_yz, 0, shard, core_dev),
        ])
        locals_.append(
            pltpu.make_async_copy(own_view(u, 0, shard), view(u, own, 0, shard), local_sem.at[u])
        )

    def begin(u):
        if u < count:
            copies[u][0].start()
            copies[u][1].start()
            copies[u][2].start()
            locals_[u].start()

    def arrive(u):
        c = copies[u]
        c[0].wait_recv()
        c[3].start()
        c[4].start()
        c[1].wait_recv()
        c[6].start()
        c[7].start()

    def relay(u):
        c = copies[u]
        c[4].wait_recv()
        c[9].start()
        c[7].wait_recv()
        c[10].start()
        c[3].wait_recv()
        c[5].start()
        c[6].wait_recv()
        c[8].start()

    def last(u):
        c = copies[u]
        c[9].wait_recv()
        c[10].wait_recv()
        c[11].start()

    def complete(u):
        c = copies[u]
        for k in (2, 5, 8, 11):
            c[k].wait_recv()
        locals_[u].wait()

    def advance(t):
        if t < count:
            arrive(t)
            begin(t + 2)
        if 0 <= t - 1 < count:
            relay(t - 1)
        if 0 <= t - 2 < count:
            last(t - 2)

    begin(0)
    begin(1)

    place = lax.broadcasted_iota(jnp.int32, (rows, rows), 0)
    column = lax.broadcasted_iota(jnp.int32, (rows, rows), 1)
    order = (column == 2 * (place % half) + place // half).astype(BF16)
    frames = jnp.dot(order, frames_ref[...], preferred_element_type=F32)
    residual[...] = frames
    normed_in[...] = norm_rows(
        frames, gain1_ref[...].astype(F32), bias1_ref[...].astype(F32)
    ).astype(BF16)
    row_window = jnp.zeros((rows, rows), jnp.int32)
    column_window = jnp.zeros((rows, rows), jnp.int32)
    end = jnp.int32(0)
    for j in range(pairs_ref.shape[1]):
        end = end + pairs_ref[0, j]
        row_window += (place % half >= end).astype(jnp.int32)
        column_window += (column % half >= end).astype(jnp.int32)
    mask[...] = jnp.where(row_window == column_window, 0.0, -1e30).astype(F32)

    block = 256

    def project(unit):
        @pl.loop(0, width // block)
        def _(i):
            cols = pl.ds(pl.multiple_of(unit * width + i * block, block), block)
            qkv[:, cols] = jnp.dot(
                normed_in[...], whole_qkv[:, cols], preferred_element_type=F32
            ).astype(BF16)

    pair = 2 * HEAD
    upper = lax.broadcasted_iota(jnp.int32, (rows, pair), 1) >= HEAD

    def softmax(scores):
        scores = scores * HEAD ** (-0.5) + mask[...]
        powers = jnp.exp(scores - jnp.max(scores, axis=1, keepdims=True))
        return (powers * (1.0 / jnp.sum(powers, axis=1, keepdims=True))).astype(BF16)

    def heads(low, high):
        @pl.loop(low, high)
        def _(i):
            at = pl.multiple_of(i * pair, pair)
            queries = qkv[:, pl.ds(at, pair)]
            keys = qkv[:, pl.ds(pl.multiple_of(width + at, pair), pair)]
            values = qkv[:, pl.ds(pl.multiple_of(2 * width + at, pair), pair)]
            results = []
            for part in (0, 1):
                chosen = jnp.where(upper == (part == 1), queries, jnp.zeros_like(queries))
                scores = lax.dot_general(
                    chosen, keys, (((1,), (1,)), ((), ())), preferred_element_type=F32
                )
                results.append(jnp.dot(softmax(scores), values, preferred_element_type=F32))
            attended[:, pl.ds(at, pair)] = jnp.where(upper, results[1], results[0]).astype(BF16)

    total = width // pair
    advance(0)
    advance(1)
    advance(2)
    complete(0)
    project(0)
    advance(3)
    complete(1)
    project(1)
    advance(4)
    complete(2)
    project(2)
    heads(0, total // 2)
    advance(5)
    heads(total // 2, total)
    advance(6)
    complete(3)

    @pl.loop(0, width // block)
    def _(i):
        cols = pl.ds(pl.multiple_of(i * block, block), block)
        residual[:, cols] += jnp.dot(
            attended[...], whole_out[:, cols], preferred_element_type=F32
        )

    pooled = (residual[0:half, :] + residual[half:rows, :]) * 0.5
    normed_ref[...] = norm_rows(
        pooled, gain2_ref[...].astype(F32), bias2_ref[...].astype(F32)
    ).astype(BF16)
    for t in range(7, count + 2):
        advance(t)
    for u in range(4, count):
        complete(u)
    for u in range(count):
        for k in range(12):
            copies[u][k].wait_send()


def project_kernel(
    rows_ref, valid_ref, w_ref, b_ref, text_ref, gain_ref, gain_tile_ref, out_ref, embed, squares
):
    j = pl.program_id(0)
    steps = pl.num_programs(0)
    slots = rows_ref.shape[0]
    columns = w_ref.shape[1]
    lines = text_ref.shape[0]
    product = jnp.dot(rows_ref[...], w_ref[...], preferred_element_type=F32)
    product = (product + b_ref[...].astype(F32)).astype(BF16)
    product = jnp.where(valid_ref[...] > 0, product.astype(F32), 0.0)

    @pl.when(j == 0)
    def _():
        squares[...] = jnp.zeros_like(squares)

    squares[...] += jnp.sum(product * product, axis=1, keepdims=True)
    embed[:, pl.ds(pl.multiple_of(j * columns, columns), columns)] = (
        product * gain_tile_ref[...].astype(F32)
    )
    text = text_ref[...].astype(F32)
    mean = jnp.mean(text * text, axis=1, keepdims=True)
    out_ref[pl.ds(pl.multiple_of(slots + j * lines, lines), lines), :] = (
        text * lax.rsqrt(mean + 1e-06) * gain_ref[...].astype(F32)
    ).astype(BF16)

    @pl.when(j == steps - 1)
    def _():
        scale = lax.rsqrt(squares[...] / embed.shape[1] + 1e-06)
        out_ref[0:slots, :] = (embed[...] * scale).astype(BF16)


def body(
    frames, ln1_gain, ln1_bias, w_qkv, w_out, ln2_gain, ln2_bias, w_proj, b_proj,
    text_embed, rms_gain, window_pairs, row_route,
):
    rows, width = frames.shape
    devices = lax.axis_size("req")
    my_index = lax.axis_index("req")
    pooled_rows = rows // 2
    capacity = 2 * pooled_rows // devices
    slots = devices * capacity
    out_width = w_proj.shape[1]
    full = GROUP * w_qkv.shape[0]
    vmem = pl.BlockSpec(memory_space=pltpu.VMEM)
    hbm = pl.BlockSpec(memory_space=pl.ANY)
    units = 8
    normed, whole_proj = pl.pallas_call(
        encoder_kernel,
        out_shape=(
            jax.ShapeDtypeStruct((pooled_rows, width), BF16),
            jax.ShapeDtypeStruct((full, out_width), BF16),
        ),
        in_specs=[vmem] * 5 + [pl.BlockSpec(memory_space=pltpu.SMEM)] + [hbm] * 3,
        out_specs=(vmem, hbm),
        scratch_shapes=[
            pltpu.VMEM((full, 3 * width), BF16),
            pltpu.VMEM((full, width), BF16),
            pltpu.VMEM((rows, width), BF16),
            pltpu.VMEM((rows, width), F32),
            pltpu.VMEM((rows, 3 * width), BF16),
            pltpu.VMEM((rows, width), BF16),
            pltpu.VMEM((rows, rows), F32),
            pltpu.SemaphoreType.DMA((units, 12)),
            pltpu.SemaphoreType.DMA((units, 12)),
            pltpu.SemaphoreType.DMA((units,)),
        ],
        compiler_params=pltpu.CompilerParams(
            collective_id=0, has_side_effects=True, vmem_limit_bytes=50 * 2**20
        ),
        name="encoder",
    )(
        frames, ln1_gain[None], ln1_bias[None], ln2_gain[None], ln2_bias[None], window_pairs,
        w_qkv, w_out, w_proj,
    )
    route_table = row_route[:, 0].reshape(devices, pooled_rows)
    own_dest = lax.dynamic_index_in_dim(route_table, my_index, 0, keepdims=False)
    one_hot = (own_dest[:, None] == jnp.arange(devices, dtype=jnp.int32)[None, :]).astype(jnp.int32)
    slot_index = jnp.sum((jnp.cumsum(one_hot, axis=0) - one_hot) * one_hot, axis=1)
    target = own_dest * capacity + slot_index
    picker = (jnp.arange(slots, dtype=jnp.int32)[:, None] == target[None, :]).astype(BF16)
    arriving = jnp.sum((route_table == my_index).astype(jnp.int32), axis=1)
    valid = jnp.arange(capacity, dtype=jnp.int32)[None, :] < arriving[:, None]
    valid = valid.astype(F32).reshape(slots, 1)
    buffer = jnp.dot(picker, normed, preferred_element_type=F32).astype(BF16)
    arrived = lax.all_to_all(
        buffer.reshape(devices, capacity, width), "req", split_axis=0, concat_axis=0, tiled=True
    ).reshape(slots, width)
    steps = 8
    columns = out_width // steps
    text_rows = text_embed.shape[0]
    return pl.pallas_call(
        project_kernel,
        grid=(steps,),
        out_shape=jax.ShapeDtypeStruct((slots + text_rows, out_width), BF16),
        in_specs=[
            pl.BlockSpec((slots, width), lambda j: (0, 0)),
            pl.BlockSpec((slots, 1), lambda j: (0, 0)),
            pl.BlockSpec((full, columns), lambda j: (0, j)),
            pl.BlockSpec((1, columns), lambda j: (0, j)),
            pl.BlockSpec((text_rows // steps, out_width), lambda j: (j, 0)),
            pl.BlockSpec((1, out_width), lambda j: (0, 0)),
            pl.BlockSpec((1, columns), lambda j: (0, j)),
        ],
        out_specs=pl.BlockSpec((slots + text_rows, out_width), lambda j: (0, 0)),
        scratch_shapes=[pltpu.VMEM((slots, out_width), F32), pltpu.VMEM((slots, 1), F32)],
        compiler_params=pltpu.CompilerParams(vmem_limit_bytes=40 * 2**20),
        name="projector",
    )(arrived, valid, whole_proj, b_proj[None], text_embed, rms_gain[None], rms_gain[None])


def solution(mesh):
    in_specs = (
        P(("groups", "req"), None),
        P(),
        P(),
        P("req", None),
        P("req", None),
        P(),
        P(),
        P("req", None),
        P(),
        P(("groups", "req"), None),
        P(),
        P(("groups", "req"), None),
        P("groups", None),
    )
    out_specs = P(("groups", "req"), None)
    return jax.shard_map(body, mesh=mesh, in_specs=in_specs, out_specs=out_specs, check_vma=False)
```

```python
import jax
import jax.numpy as jnp
from jax import lax
from jax.experimental import pallas as pl
from jax.experimental.pallas import tpu as pltpu
from jax.sharding import PartitionSpec as P

HEAD = 64
GROUP = 8
MESH = pl.DeviceIdType.MESH
F32 = jnp.float32
BF16 = jnp.bfloat16


def flipped(index, bit):
    return index + bit - 2 * bit * ((index // bit) % 2)


def norm_rows(values, gain, bias):
    mean = jnp.mean(values, axis=-1, keepdims=True)
    centered = values - mean
    variance = jnp.mean(centered * centered, axis=-1, keepdims=True)
    return centered * lax.rsqrt(variance + 1e-05) * gain + bias


def encoder_kernel(
    frames_hbm, gain1_hbm, bias1_hbm, gain2_hbm, bias2_hbm, b_proj_hbm, pairs_hbm, route_ref,
    qkv_ref, out_w_ref, proj_ref,
    embed_ref,
    whole_qkv, whole_out, whole_proj, frames_ref, gain1_ref, bias1_ref, gain2_ref, bias2_ref,
    b_proj_ref, b_row, pairs_ref, normed_in, residual, qkv, attended, mask, buffer, arrived, packed,
    send_sem, recv_sem, local_sem, load_sem, rows_send, rows_recv,
):
    width = frames_ref.shape[1]
    rows = frames_ref.shape[0]
    half = rows // 2
    shard = qkv_ref.shape[0]
    g = lax.axis_index("groups")
    r = lax.axis_index("req")
    lane = g % 2
    mine = r % GROUP
    core_dev = (g, flipped(r, 1))
    y_dev = (g, flipped(r, 2))
    z_dev = (g, flipped(r, 4))
    x_dev = (flipped(g, 1), r)
    own = mine
    from_y = flipped(mine, 2)
    from_z = flipped(mine, 4)
    from_yz = flipped(from_y, 4)

    barrier = pltpu.get_barrier_semaphore()
    devices = route_ref.shape[0]

    @pl.loop(1, devices)
    def _(i):
        pl.semaphore_signal(
            barrier, inc=1, device_id=(g, (r + i) % devices), device_id_type=MESH
        )

    pl.semaphore_signal(barrier, inc=1, device_id=x_dev, device_id_type=MESH)
    loads = [
        pltpu.make_async_copy(source, target, load_sem.at[k])
        for k, (source, target) in enumerate([
            (frames_hbm, frames_ref), (gain1_hbm, gain1_ref), (bias1_hbm, bias1_ref),
            (gain2_hbm, gain2_ref), (bias2_hbm, bias2_ref), (b_proj_hbm, b_proj_ref),
            (pairs_hbm, pairs_ref),
        ])
    ]
    for load in loads:
        load.start()
    pl.semaphore_wait(barrier, devices)

    pieces = 4
    proj_cols = proj_ref.shape[1] // pieces
    units = [(qkv_ref, whole_qkv, j * width, width) for j in range(3)]
    units.append((out_w_ref, whole_out, 0, width))
    units += [(proj_ref, whole_proj, j * proj_cols, proj_cols) for j in range(pieces)]
    count = len(units)
    tile = 16
    step = shard // (5 * tile) * tile
    direct = shard - step
    middle = shard // 2
    first = middle // tile // 2 * tile
    second = middle - first

    def view(unit, block, start, size):
        _, whole, column, columns = units[unit]
        begin = pl.multiple_of(block * shard + start, tile)
        return whole.at[pl.ds(begin, size), pl.ds(column, columns)]

    def own_view(unit, start, size):
        source, _, column, columns = units[unit]
        return source.at[pl.ds(pl.multiple_of(start, tile), size), pl.ds(column, columns)]

    def remote(unit, which, source, target, device):
        return pltpu.make_async_remote_copy(
            src_ref=source,
            dst_ref=target,
            send_sem=send_sem.at[unit, which],
            recv_sem=recv_sem.at[unit, which],
            device_id=device,
            device_id_type=MESH,
        )

    def moved(unit, which, block, start, size, device):
        span = view(unit, block, start, size)
        return remote(unit, which, span, span, device)

    def split(unit):
        return (second, first) if unit % 2 else (first, second)

    copies = []
    locals_ = []
    for u in range(count):
        via_y, via_z = split(u)
        d0 = lane * step
        m0 = lane * middle
        copies.append([
            remote(u, 0, own_view(u, d0, direct), view(u, own, d0, direct), y_dev),
            remote(u, 1, own_view(u, d0, direct), view(u, own, d0, direct), z_dev),
            remote(u, 2, own_view(u, 0, shard), view(u, own, 0, shard), core_dev),
            moved(u, 3, from_y, lane * direct, step, x_dev),
            moved(u, 4, from_y, m0 + via_y, via_z, z_dev),
            moved(u, 5, from_y, 0, shard, core_dev),
            moved(u, 6, from_z, lane * direct, step, x_dev),
            moved(u, 7, from_z, m0, via_y, y_dev),
            moved(u, 8, from_z, 0, shard, core_dev),
            moved(u, 9, from_yz, m0 + via_y, via_z, x_dev),
            moved(u, 10, from_yz, m0, via_y, x_dev),
            moved(u, 11, from_yz, 0, shard, core_dev),
        ])
        locals_.append(
            pltpu.make_async_copy(own_view(u, 0, shard), view(u, own, 0, shard), local_sem.at[u])
        )

    def begin(u):
        if u < count:
            copies[u][0].start()
            copies[u][1].start()
            copies[u][2].start()
            locals_[u].start()

    def arrive(u):
        c = copies[u]
        c[0].wait_recv()
        c[3].start()
        c[4].start()
        c[1].wait_recv()
        c[6].start()
        c[7].start()

    def relay(u):
        c = copies[u]
        c[4].wait_recv()
        c[9].start()
        c[7].wait_recv()
        c[10].start()
        c[3].wait_recv()
        c[5].start()
        c[6].wait_recv()
        c[8].start()

    def last(u):
        c = copies[u]
        c[9].wait_recv()
        c[10].wait_recv()
        c[11].start()

    def complete(u):
        c = copies[u]
        for k in (2, 5, 8, 11):
            c[k].wait_recv()
        locals_[u].wait()

    def advance(t):
        if t < count:
            arrive(t)
            begin(t + 2)
        if 0 <= t - 1 < count:
            relay(t - 1)
        if 0 <= t - 2 < count:
            last(t - 2)

    begin(0)
    begin(1)
    for load in loads:
        load.wait()

    def row_of(ref):
        return ref[...].reshape(1, ref.shape[0]).astype(F32)

    b_row[...] = row_of(b_proj_ref)
    place = lax.broadcasted_iota(jnp.int32, (rows, rows), 0)
    column = lax.broadcasted_iota(jnp.int32, (rows, rows), 1)
    order = (column == 2 * (place % half) + place // half).astype(BF16)
    frames = jnp.dot(order, frames_ref[...], preferred_element_type=F32)
    residual[...] = frames
    normed_in[...] = norm_rows(
        frames, row_of(gain1_ref), row_of(bias1_ref)
    ).astype(BF16)
    row_window = jnp.zeros((rows, rows), jnp.int32)
    column_window = jnp.zeros((rows, rows), jnp.int32)
    end = jnp.int32(0)
    for j in range(pairs_ref.shape[1]):
        end = end + pairs_ref[0, j]
        row_window += (place % half >= end).astype(jnp.int32)
        column_window += (column % half >= end).astype(jnp.int32)
    mask[...] = jnp.where(row_window == column_window, 0.0, -1e30).astype(F32)

    block = 256

    def project(unit):
        @pl.loop(0, width // block)
        def _(i):
            cols = pl.ds(pl.multiple_of(unit * width + i * block, block), block)
            qkv[:, cols] = jnp.dot(
                normed_in[...], whole_qkv[:, cols], preferred_element_type=F32
            ).astype(BF16)

    pair = 2 * HEAD
    upper = lax.broadcasted_iota(jnp.int32, (rows, pair), 1) >= HEAD

    def softmax(scores):
        scores = scores * HEAD ** (-0.5) + mask[...]
        powers = jnp.exp(scores - jnp.max(scores, axis=1, keepdims=True))
        return (powers * (1.0 / jnp.sum(powers, axis=1, keepdims=True))).astype(BF16)

    def heads(low, high):
        @pl.loop(low, high)
        def _(i):
            at = pl.multiple_of(i * pair, pair)
            queries = qkv[:, pl.ds(at, pair)]
            keys = qkv[:, pl.ds(pl.multiple_of(width + at, pair), pair)]
            values = qkv[:, pl.ds(pl.multiple_of(2 * width + at, pair), pair)]
            results = []
            for part in (0, 1):
                chosen = jnp.where(upper == (part == 1), queries, jnp.zeros_like(queries))
                scores = lax.dot_general(
                    chosen, keys, (((1,), (1,)), ((), ())), preferred_element_type=F32
                )
                results.append(jnp.dot(softmax(scores), values, preferred_element_type=F32))
            attended[:, pl.ds(at, pair)] = jnp.where(upper, results[1], results[0]).astype(BF16)

    total = width // pair
    advance(0)
    advance(1)
    advance(2)
    complete(0)
    project(0)
    advance(3)
    complete(1)
    project(1)
    advance(4)
    complete(2)
    project(2)
    heads(0, total // 2)
    advance(5)
    heads(total // 2, total)
    advance(6)
    complete(3)

    @pl.loop(0, width // block)
    def _(i):
        cols = pl.ds(pl.multiple_of(i * block, block), block)
        residual[:, cols] += jnp.dot(
            attended[...], whole_out[:, cols], preferred_element_type=F32
        )

    pooled = (residual[0:half, :] + residual[half:rows, :]) * 0.5
    normed = norm_rows(pooled, row_of(gain2_ref), row_of(bias2_ref)).astype(BF16)
    capacity = 2 * half // devices
    stride = buffer.shape[0] // devices
    across = lax.broadcasted_iota(jnp.int32, (half, half), 1)
    down = lax.broadcasted_iota(jnp.int32, (half, half), 0)
    dest = route_ref[pl.ds(r, 1), :].astype(F32)
    dest_down = jnp.sum(jnp.where(across == down, dest, 0.0), axis=1, keepdims=True)
    earlier = jnp.where((dest_down == dest) & (down < across), 1.0, 0.0)
    target = dest * stride + jnp.sum(earlier, axis=0, keepdims=True)
    slot = lax.broadcasted_iota(jnp.int32, (buffer.shape[0], half), 0)
    picker = (slot == target.astype(jnp.int32)).astype(BF16)
    buffer[...] = jnp.dot(picker, normed, preferred_element_type=F32).astype(BF16)

    def exchange(i):
        to = (r + i) % devices
        return pltpu.make_async_remote_copy(
            src_ref=buffer.at[pl.ds(pl.multiple_of(to * stride, tile), stride), :],
            dst_ref=arrived.at[pl.ds(pl.multiple_of(r * stride, tile), stride), :],
            send_sem=rows_send.at[i],
            recv_sem=rows_recv.at[i],
            device_id=(g, to),
            device_id_type=MESH,
        )

    @pl.loop(1, devices)
    def _(i):
        exchange(i).start()

    mine_rows = pl.ds(pl.multiple_of(r * stride, tile), stride)
    stay = pltpu.make_async_copy(
        buffer.at[mine_rows, :], arrived.at[mine_rows, :], local_sem.at[count]
    )
    stay.start()
    advance(7)
    advance(8)

    @pl.loop(1, devices)
    def _(i):
        exchange(i).wait_recv()

    stay.wait()
    slots = devices * capacity
    if capacity == stride:
        packed[...] = arrived[...]
    else:
        row = lax.broadcasted_iota(jnp.int32, (slots, devices * stride), 0)
        wide = lax.broadcasted_iota(jnp.int32, (slots, devices * stride), 1)
        keep = (wide == row // capacity * stride + row % capacity).astype(BF16)
        packed[...] = jnp.dot(keep, arrived[...], preferred_element_type=F32).astype(BF16)
    sender = lax.broadcasted_iota(jnp.int32, (slots, devices), 1)
    place = lax.broadcasted_iota(jnp.int32, (slots, devices), 0)
    spread = (place // capacity == sender).astype(BF16)
    named = jnp.where(route_ref[...] == r, 1.0, 0.0).astype(BF16)
    filled = jnp.sum(
        jnp.dot(spread, named, preferred_element_type=F32), axis=1, keepdims=True
    )
    order = lax.broadcasted_iota(jnp.int32, (slots, 1), 0) % capacity
    valid = order.astype(F32) < filled

    def embed(piece):
        @pl.loop(0, proj_cols // block)
        def _(i):
            cols = pl.ds(pl.multiple_of(piece * proj_cols + i * block, block), block)
            product = jnp.dot(packed[...], whole_proj[:, cols], preferred_element_type=F32)
            embed_ref[:, cols] = jnp.where(valid, product + b_row[:, cols], 0.0).astype(BF16)

    complete(4)
    embed(0)
    complete(5)
    embed(1)
    advance(9)
    complete(6)
    embed(2)
    complete(7)
    embed(3)
    for u in range(count):
        for k in range(12):
            copies[u][k].wait_send()

    @pl.loop(1, devices)
    def _(i):
        exchange(i).wait_send()


def rms_kernel(audio_ref, text_ref, gain_ref, out_ref):
    j = pl.program_id(0)
    steps = pl.num_programs(0) // 2

    def write(ref):
        values = ref[...].astype(F32)
        mean = jnp.mean(values * values, axis=1, keepdims=True)
        out_ref[...] = (values * lax.rsqrt(mean + 1e-06) * gain_ref[...].astype(F32)).astype(BF16)

    @pl.when(j < steps)
    def _():
        write(audio_ref)

    @pl.when(j >= steps)
    def _():
        write(text_ref)


def body(
    frames, ln1_gain, ln1_bias, w_qkv, w_out, ln2_gain, ln2_bias, w_proj, b_proj,
    text_embed, rms_gain, window_pairs, row_route,
):
    rows, width = frames.shape
    devices = lax.axis_size("req")
    pooled_rows = rows // 2
    capacity = 2 * pooled_rows // devices
    slots = devices * capacity
    out_width = w_proj.shape[1]
    full = GROUP * w_qkv.shape[0]
    vmem = pl.BlockSpec(memory_space=pltpu.VMEM)
    hbm = pl.BlockSpec(memory_space=pl.ANY)
    units = 8
    stride = max(capacity, 16)
    route_table = row_route.reshape(devices, pooled_rows)
    embed = pl.pallas_call(
        encoder_kernel,
        out_shape=jax.ShapeDtypeStruct((slots, out_width), BF16),
        in_specs=[hbm] * 7 + [vmem] + [hbm] * 3,
        out_specs=vmem,
        scratch_shapes=[
            pltpu.VMEM((full, 3 * width), BF16),
            pltpu.VMEM((full, width), BF16),
            pltpu.VMEM((full, out_width), BF16),
            pltpu.VMEM((rows, width), BF16),
            pltpu.VMEM((width,), BF16),
            pltpu.VMEM((width,), BF16),
            pltpu.VMEM((width,), BF16),
            pltpu.VMEM((width,), BF16),
            pltpu.VMEM((out_width,), BF16),
            pltpu.VMEM((1, out_width), F32),
            pltpu.SMEM(window_pairs.shape, jnp.int32),
            pltpu.VMEM((rows, width), BF16),
            pltpu.VMEM((rows, width), F32),
            pltpu.VMEM((rows, 3 * width), BF16),
            pltpu.VMEM((rows, width), BF16),
            pltpu.VMEM((rows, rows), F32),
            pltpu.VMEM((devices * stride, width), BF16),
            pltpu.VMEM((devices * stride, width), BF16),
            pltpu.VMEM((slots, width), BF16),
            pltpu.SemaphoreType.DMA((units, 12)),
            pltpu.SemaphoreType.DMA((units, 12)),
            pltpu.SemaphoreType.DMA((units + 1,)),
            pltpu.SemaphoreType.DMA((7,)),
            pltpu.SemaphoreType.DMA((devices,)),
            pltpu.SemaphoreType.DMA((devices,)),
        ],
        compiler_params=pltpu.CompilerParams(
            collective_id=0, has_side_effects=True, vmem_limit_bytes=58 * 2**20
        ),
        name="encoder",
    )(
        frames, ln1_gain, ln1_bias, ln2_gain, ln2_bias, b_proj, window_pairs, route_table,
        w_qkv, w_out, w_proj,
    )
    text_rows = text_embed.shape[0]
    steps = 4
    audio_block = slots // steps
    return pl.pallas_call(
        rms_kernel,
        grid=(2 * steps,),
        out_shape=jax.ShapeDtypeStruct((slots + text_rows, out_width), BF16),
        in_specs=[
            pl.BlockSpec((audio_block, out_width), lambda j: (jnp.minimum(j, steps - 1), 0)),
            pl.BlockSpec((audio_block, out_width), lambda j: (jnp.maximum(j - steps, 0), 0)),
            pl.BlockSpec((1, out_width), lambda j: (0, 0)),
        ],
        out_specs=pl.BlockSpec((audio_block, out_width), lambda j: (j, 0)),
        compiler_params=pltpu.CompilerParams(vmem_limit_bytes=58 * 2**20),
        name="rms",
    )(embed, text_embed, rms_gain[None])


def solution(mesh):
    in_specs = (
        P(("groups", "req"), None),
        P(),
        P(),
        P("req", None),
        P("req", None),
        P(),
        P(),
        P("req", None),
        P(),
        P(("groups", "req"), None),
        P(),
        P(("groups", "req"), None),
        P("groups", None),
    )
    out_specs = P(("groups", "req"), None)
    return jax.shard_map(body, mesh=mesh, in_specs=in_specs, out_specs=out_specs, check_vma=False)
```

```python
import jax
import jax.numpy as jnp
from jax import lax
from jax.experimental import pallas as pl
from jax.experimental.pallas import tpu as pltpu
from jax.sharding import PartitionSpec as P

HEAD = 64
GROUP = 8
MESH = pl.DeviceIdType.MESH
F32 = jnp.float32
BF16 = jnp.bfloat16


def flipped(index, bit):
    return index + bit - 2 * bit * ((index // bit) % 2)


def norm_rows(values, gain, bias):
    mean = jnp.mean(values, axis=-1, keepdims=True)
    centered = values - mean
    variance = jnp.mean(centered * centered, axis=-1, keepdims=True)
    return centered * lax.rsqrt(variance + 1e-05) * gain + bias


def encoder_kernel(
    frames_hbm, gain1_hbm, bias1_hbm, gain2_hbm, bias2_hbm, b_proj_hbm, pairs_hbm, route_ref,
    qkv_ref, out_w_ref, proj_ref,
    embed_ref,
    whole_qkv, whole_out, whole_proj, frames_ref, gain1_ref, bias1_ref, gain2_ref, bias2_ref,
    b_proj_ref, b_row, pairs_ref, normed_in, residual, qkv, attended, mask, buffer, arrived, packed,
    send_sem, recv_sem, local_sem, load_sem, rows_send, rows_recv,
):
    width = frames_ref.shape[1]
    rows = frames_ref.shape[0]
    half = rows // 2
    shard = qkv_ref.shape[0]
    g = lax.axis_index("groups")
    r = lax.axis_index("req")
    lane = g % 2
    mine = r % GROUP
    core_dev = (g, flipped(r, 1))
    y_dev = (g, flipped(r, 2))
    z_dev = (g, flipped(r, 4))
    x_dev = (flipped(g, 1), r)
    own = mine
    from_y = flipped(mine, 2)
    from_z = flipped(mine, 4)
    from_yz = flipped(from_y, 4)

    barrier = pltpu.get_barrier_semaphore()
    devices = route_ref.shape[0]

    @pl.loop(1, devices)
    def _(i):
        pl.semaphore_signal(
            barrier, inc=1, device_id=(g, (r + i) % devices), device_id_type=MESH
        )

    pl.semaphore_signal(barrier, inc=1, device_id=x_dev, device_id_type=MESH)
    loads = [
        pltpu.make_async_copy(source, target, load_sem.at[k])
        for k, (source, target) in enumerate([
            (frames_hbm, frames_ref), (gain1_hbm, gain1_ref), (bias1_hbm, bias1_ref),
            (gain2_hbm, gain2_ref), (bias2_hbm, bias2_ref), (b_proj_hbm, b_proj_ref),
            (pairs_hbm, pairs_ref),
        ])
    ]
    for load in loads:
        load.start()
    pl.semaphore_wait(barrier, devices)

    pieces = 4
    proj_cols = proj_ref.shape[1] // pieces
    units = [(qkv_ref, whole_qkv, j * width, width) for j in range(3)]
    units.append((out_w_ref, whole_out, 0, width))
    units += [(proj_ref, whole_proj, j * proj_cols, proj_cols) for j in range(pieces)]
    count = len(units)
    tile = 16
    step = shard // (5 * tile) * tile
    direct = shard - step
    middle = shard // 2
    first = middle // tile // 2 * tile
    second = middle - first

    def view(unit, block, start, size):
        _, whole, column, columns = units[unit]
        begin = pl.multiple_of(block * shard + start, tile)
        return whole.at[pl.ds(begin, size), pl.ds(column, columns)]

    def own_view(unit, start, size):
        source, _, column, columns = units[unit]
        return source.at[pl.ds(pl.multiple_of(start, tile), size), pl.ds(column, columns)]

    def remote(unit, which, source, target, device):
        return pltpu.make_async_remote_copy(
            src_ref=source,
            dst_ref=target,
            send_sem=send_sem.at[unit, which],
            recv_sem=recv_sem.at[unit, which],
            device_id=device,
            device_id_type=MESH,
        )

    def moved(unit, which, block, start, size, device):
        span = view(unit, block, start, size)
        return remote(unit, which, span, span, device)

    def split(unit):
        return (second, first) if unit % 2 else (first, second)

    copies = []
    locals_ = []
    for u in range(count):
        via_y, via_z = split(u)
        d0 = lane * step
        m0 = lane * middle
        copies.append([
            remote(u, 0, own_view(u, d0, direct), view(u, own, d0, direct), y_dev),
            remote(u, 1, own_view(u, d0, direct), view(u, own, d0, direct), z_dev),
            remote(u, 2, own_view(u, 0, shard), view(u, own, 0, shard), core_dev),
            moved(u, 3, from_y, lane * direct, step, x_dev),
            moved(u, 4, from_y, m0 + via_y, via_z, z_dev),
            moved(u, 5, from_y, 0, shard, core_dev),
            moved(u, 6, from_z, lane * direct, step, x_dev),
            moved(u, 7, from_z, m0, via_y, y_dev),
            moved(u, 8, from_z, 0, shard, core_dev),
            moved(u, 9, from_yz, m0 + via_y, via_z, x_dev),
            moved(u, 10, from_yz, m0, via_y, x_dev),
            moved(u, 11, from_yz, 0, shard, core_dev),
        ])
        locals_.append(
            pltpu.make_async_copy(own_view(u, 0, shard), view(u, own, 0, shard), local_sem.at[u])
        )

    def begin(u):
        if u < count:
            copies[u][0].start()
            copies[u][1].start()
            copies[u][2].start()
            locals_[u].start()

    def arrive(u):
        c = copies[u]
        c[0].wait_recv()
        c[3].start()
        c[4].start()
        c[1].wait_recv()
        c[6].start()
        c[7].start()

    def relay(u):
        c = copies[u]
        c[4].wait_recv()
        c[9].start()
        c[7].wait_recv()
        c[10].start()
        c[3].wait_recv()
        c[5].start()
        c[6].wait_recv()
        c[8].start()

    def last(u):
        c = copies[u]
        c[9].wait_recv()
        c[10].wait_recv()
        c[11].start()

    def complete(u):
        c = copies[u]
        for k in (2, 5, 8, 11):
            c[k].wait_recv()
        locals_[u].wait()

    def advance(t):
        if t < count:
            arrive(t)
            begin(t + 2)
        if 0 <= t - 1 < count:
            relay(t - 1)
        if 0 <= t - 2 < count:
            last(t - 2)

    begin(0)
    begin(1)
    for load in loads:
        load.wait()

    def row_of(ref):
        return ref[...].reshape(1, ref.shape[0]).astype(F32)

    b_row[...] = row_of(b_proj_ref)
    place = lax.broadcasted_iota(jnp.int32, (rows, rows), 0)
    column = lax.broadcasted_iota(jnp.int32, (rows, rows), 1)
    order = (column == 2 * (place % half) + place // half).astype(BF16)
    frames = jnp.dot(order, frames_ref[...], preferred_element_type=F32)
    residual[...] = frames
    normed_in[...] = norm_rows(
        frames, row_of(gain1_ref), row_of(bias1_ref)
    ).astype(BF16)
    row_window = jnp.zeros((rows, rows), jnp.int32)
    column_window = jnp.zeros((rows, rows), jnp.int32)
    end = jnp.int32(0)
    for j in range(pairs_ref.shape[1]):
        end = end + pairs_ref[0, j]
        row_window += (place % half >= end).astype(jnp.int32)
        column_window += (column % half >= end).astype(jnp.int32)
    mask[...] = jnp.where(row_window == column_window, 0.0, -1e30).astype(F32)

    block = 256

    def project(unit):
        @pl.loop(0, width // block)
        def _(i):
            cols = pl.ds(pl.multiple_of(unit * width + i * block, block), block)
            qkv[:, cols] = jnp.dot(
                normed_in[...], whole_qkv[:, cols], preferred_element_type=F32
            ).astype(BF16)

    pair = 2 * HEAD
    upper = lax.broadcasted_iota(jnp.int32, (rows, pair), 1) >= HEAD

    def softmax(scores):
        scores = scores * HEAD ** (-0.5) + mask[...]
        powers = jnp.exp(scores - jnp.max(scores, axis=1, keepdims=True))
        return (powers * (1.0 / jnp.sum(powers, axis=1, keepdims=True))).astype(BF16)

    def heads(low, high):
        @pl.loop(low, high)
        def _(i):
            at = pl.multiple_of(i * pair, pair)
            queries = qkv[:, pl.ds(at, pair)]
            keys = qkv[:, pl.ds(pl.multiple_of(width + at, pair), pair)]
            values = qkv[:, pl.ds(pl.multiple_of(2 * width + at, pair), pair)]
            results = []
            for part in (0, 1):
                chosen = jnp.where(upper == (part == 1), queries, jnp.zeros_like(queries))
                scores = lax.dot_general(
                    chosen, keys, (((1,), (1,)), ((), ())), preferred_element_type=F32
                )
                results.append(jnp.dot(softmax(scores), values, preferred_element_type=F32))
            attended[:, pl.ds(at, pair)] = jnp.where(upper, results[1], results[0]).astype(BF16)

    total = width // pair
    advance(0)
    advance(1)
    advance(2)
    complete(0)
    project(0)
    advance(3)
    complete(1)
    project(1)
    advance(4)
    complete(2)
    project(2)
    heads(0, total // 2)
    advance(5)
    heads(total // 2, total)
    advance(6)
    complete(3)

    @pl.loop(0, width // block)
    def _(i):
        cols = pl.ds(pl.multiple_of(i * block, block), block)
        residual[:, cols] += jnp.dot(
            attended[...], whole_out[:, cols], preferred_element_type=F32
        )

    pooled = (residual[0:half, :] + residual[half:rows, :]) * 0.5
    normed = norm_rows(pooled, row_of(gain2_ref), row_of(bias2_ref)).astype(BF16)
    capacity = 2 * half // devices
    stride = buffer.shape[0] // devices
    across = lax.broadcasted_iota(jnp.int32, (half, half), 1)
    down = lax.broadcasted_iota(jnp.int32, (half, half), 0)
    dest = route_ref[pl.ds(r, 1), :].astype(F32)
    dest_down = jnp.sum(jnp.where(across == down, dest, 0.0), axis=1, keepdims=True)
    earlier = jnp.where((dest_down == dest) & (down < across), 1.0, 0.0)
    target = dest * stride + jnp.sum(earlier, axis=0, keepdims=True)
    slot = lax.broadcasted_iota(jnp.int32, (buffer.shape[0], half), 0)
    picker = (slot == target.astype(jnp.int32)).astype(BF16)
    buffer[...] = jnp.dot(picker, normed, preferred_element_type=F32).astype(BF16)

    def exchange(i):
        to = (r + i) % devices
        return pltpu.make_async_remote_copy(
            src_ref=buffer.at[pl.ds(pl.multiple_of(to * stride, tile), stride), :],
            dst_ref=arrived.at[pl.ds(pl.multiple_of(r * stride, tile), stride), :],
            send_sem=rows_send.at[i],
            recv_sem=rows_recv.at[i],
            device_id=(g, to),
            device_id_type=MESH,
        )

    @pl.loop(1, devices)
    def _(i):
        exchange(i).start()

    mine_rows = pl.ds(pl.multiple_of(r * stride, tile), stride)
    stay = pltpu.make_async_copy(
        buffer.at[mine_rows, :], arrived.at[mine_rows, :], local_sem.at[count]
    )
    stay.start()
    advance(7)
    advance(8)

    @pl.loop(1, devices)
    def _(i):
        exchange(i).wait_recv()

    stay.wait()
    slots = devices * capacity
    if capacity == stride:
        packed[...] = arrived[...]
    else:
        row = lax.broadcasted_iota(jnp.int32, (slots, devices * stride), 0)
        wide = lax.broadcasted_iota(jnp.int32, (slots, devices * stride), 1)
        keep = (wide == row // capacity * stride + row % capacity).astype(BF16)
        packed[...] = jnp.dot(keep, arrived[...], preferred_element_type=F32).astype(BF16)
    sender = lax.broadcasted_iota(jnp.int32, (slots, devices), 1)
    place = lax.broadcasted_iota(jnp.int32, (slots, devices), 0)
    spread = (place // capacity == sender).astype(BF16)
    named = jnp.where(route_ref[...] == r, 1.0, 0.0).astype(BF16)
    filled = jnp.sum(
        jnp.dot(spread, named, preferred_element_type=F32), axis=1, keepdims=True
    )
    order = lax.broadcasted_iota(jnp.int32, (slots, 1), 0) % capacity
    valid = order.astype(F32) < filled

    def embed(piece):
        @pl.loop(0, proj_cols // block)
        def _(i):
            cols = pl.ds(pl.multiple_of(piece * proj_cols + i * block, block), block)
            product = jnp.dot(packed[...], whole_proj[:, cols], preferred_element_type=F32)
            embed_ref[:, cols] = jnp.where(valid, product + b_row[:, cols], 0.0).astype(BF16)

    complete(4)
    embed(0)
    complete(5)
    embed(1)
    advance(9)
    complete(6)
    embed(2)
    complete(7)
    embed(3)
    for u in range(count):
        for k in range(12):
            copies[u][k].wait_send()

    @pl.loop(1, devices)
    def _(i):
        exchange(i).wait_send()


def rms_kernel(audio_ref, text_ref, gain_ref, out_ref):
    j = pl.program_id(0)
    steps = pl.num_programs(0) // 2

    def write(ref):
        values = ref[...].astype(F32)
        gain = gain_ref[...].reshape(1, gain_ref.shape[0]).astype(F32)
        mean = jnp.mean(values * values, axis=1, keepdims=True)
        out_ref[...] = (values * lax.rsqrt(mean + 1e-06) * gain).astype(BF16)

    @pl.when(j < steps)
    def _():
        write(audio_ref)

    @pl.when(j >= steps)
    def _():
        write(text_ref)


def body(
    frames, ln1_gain, ln1_bias, w_qkv, w_out, ln2_gain, ln2_bias, w_proj, b_proj,
    text_embed, rms_gain, window_pairs, row_route,
):
    rows, width = frames.shape
    devices = lax.axis_size("req")
    pooled_rows = rows // 2
    capacity = 2 * pooled_rows // devices
    slots = devices * capacity
    out_width = w_proj.shape[1]
    full = GROUP * w_qkv.shape[0]
    vmem = pl.BlockSpec(memory_space=pltpu.VMEM)
    hbm = pl.BlockSpec(memory_space=pl.ANY)
    units = 8
    stride = max(capacity, 16)
    route_table = row_route.reshape(devices, pooled_rows)
    embed = pl.pallas_call(
        encoder_kernel,
        out_shape=jax.ShapeDtypeStruct((slots, out_width), BF16),
        in_specs=[hbm] * 7 + [vmem] + [hbm] * 3,
        out_specs=vmem,
        scratch_shapes=[
            pltpu.VMEM((full, 3 * width), BF16),
            pltpu.VMEM((full, width), BF16),
            pltpu.VMEM((full, out_width), BF16),
            pltpu.VMEM((rows, width), BF16),
            pltpu.VMEM((width,), BF16),
            pltpu.VMEM((width,), BF16),
            pltpu.VMEM((width,), BF16),
            pltpu.VMEM((width,), BF16),
            pltpu.VMEM((out_width,), BF16),
            pltpu.VMEM((1, out_width), F32),
            pltpu.SMEM(window_pairs.shape, jnp.int32),
            pltpu.VMEM((rows, width), BF16),
            pltpu.VMEM((rows, width), F32),
            pltpu.VMEM((rows, 3 * width), BF16),
            pltpu.VMEM((rows, width), BF16),
            pltpu.VMEM((rows, rows), F32),
            pltpu.VMEM((devices * stride, width), BF16),
            pltpu.VMEM((devices * stride, width), BF16),
            pltpu.VMEM((slots, width), BF16),
            pltpu.SemaphoreType.DMA((units, 12)),
            pltpu.SemaphoreType.DMA((units, 12)),
            pltpu.SemaphoreType.DMA((units + 1,)),
            pltpu.SemaphoreType.DMA((7,)),
            pltpu.SemaphoreType.DMA((devices,)),
            pltpu.SemaphoreType.DMA((devices,)),
        ],
        compiler_params=pltpu.CompilerParams(
            collective_id=0, has_side_effects=True, vmem_limit_bytes=58 * 2**20
        ),
        name="encoder",
    )(
        frames, ln1_gain, ln1_bias, ln2_gain, ln2_bias, b_proj, window_pairs, route_table,
        w_qkv, w_out, w_proj,
    )
    text_rows = text_embed.shape[0]
    steps = 2
    audio_block = slots // steps
    return pl.pallas_call(
        rms_kernel,
        grid=(2 * steps,),
        out_shape=jax.ShapeDtypeStruct((slots + text_rows, out_width), BF16),
        in_specs=[
            pl.BlockSpec((audio_block, out_width), lambda j: (jnp.minimum(j, steps - 1), 0)),
            pl.BlockSpec((audio_block, out_width), lambda j: (jnp.maximum(j - steps, 0), 0)),
            pl.BlockSpec((out_width,), lambda j: (0,)),
        ],
        out_specs=pl.BlockSpec((audio_block, out_width), lambda j: (j, 0)),
        compiler_params=pltpu.CompilerParams(vmem_limit_bytes=58 * 2**20),
        name="rms",
    )(embed, text_embed, rms_gain)


def solution(mesh):
    in_specs = (
        P(("groups", "req"), None),
        P(),
        P(),
        P("req", None),
        P("req", None),
        P(),
        P(),
        P("req", None),
        P(),
        P(("groups", "req"), None),
        P(),
        P(("groups", "req"), None),
        P("groups", None),
    )
    out_specs = P(("groups", "req"), None)
    return jax.shard_map(body, mesh=mesh, in_specs=in_specs, out_specs=out_specs, check_vma=False)
```

```python
import jax
import jax.numpy as jnp
from jax import lax
from jax.experimental import pallas as pl
from jax.experimental.pallas import tpu as pltpu
from jax.sharding import PartitionSpec as P

HEAD = 64
GROUP = 8
MESH = pl.DeviceIdType.MESH
F32 = jnp.float32
BF16 = jnp.bfloat16


def flipped(index, bit):
    return index + bit - 2 * bit * ((index // bit) % 2)


def norm_rows(values, gain, bias):
    mean = jnp.mean(values, axis=-1, keepdims=True)
    centered = values - mean
    variance = jnp.mean(centered * centered, axis=-1, keepdims=True)
    return centered * lax.rsqrt(variance + 1e-05) * gain + bias


def encoder_kernel(
    frames_hbm, gain1_hbm, bias1_hbm, gain2_hbm, bias2_hbm, b_proj_hbm, pairs_hbm, route_ref,
    qkv_ref, out_w_ref, proj_ref,
    embed_ref,
    whole_qkv, whole_out, whole_proj, frames_ref, gain1_ref, bias1_ref, gain2_ref, bias2_ref,
    b_proj_ref, b_row, pairs_ref, normed_in, residual, qkv, attended, mask, buffer, arrived, packed,
    send_sem, recv_sem, local_sem, load_sem, rows_send, rows_recv,
):
    width = frames_ref.shape[1]
    rows = frames_ref.shape[0]
    half = rows // 2
    shard = qkv_ref.shape[0]
    g = lax.axis_index("groups")
    r = lax.axis_index("req")
    lane = g % 2
    mine = r % GROUP
    core_dev = (g, flipped(r, 1))
    y_dev = (g, flipped(r, 2))
    z_dev = (g, flipped(r, 4))
    x_dev = (flipped(g, 1), r)
    own = mine
    from_y = flipped(mine, 2)
    from_z = flipped(mine, 4)
    from_yz = flipped(from_y, 4)

    barrier = pltpu.get_barrier_semaphore()
    devices = route_ref.shape[0]

    @pl.loop(1, devices)
    def _(i):
        pl.semaphore_signal(
            barrier, inc=1, device_id=(g, (r + i) % devices), device_id_type=MESH
        )

    pl.semaphore_signal(barrier, inc=1, device_id=x_dev, device_id_type=MESH)
    loads = [
        pltpu.make_async_copy(source, target, load_sem.at[k])
        for k, (source, target) in enumerate([
            (frames_hbm, frames_ref), (gain1_hbm, gain1_ref), (bias1_hbm, bias1_ref),
            (gain2_hbm, gain2_ref), (bias2_hbm, bias2_ref), (b_proj_hbm, b_proj_ref),
            (pairs_hbm, pairs_ref),
        ])
    ]
    for load in loads:
        load.start()
    pl.semaphore_wait(barrier, devices)

    pieces = 4
    proj_cols = proj_ref.shape[1] // pieces
    units = [(qkv_ref, whole_qkv, j * width, width) for j in range(3)]
    units.append((out_w_ref, whole_out, 0, width))
    units += [(proj_ref, whole_proj, j * proj_cols, proj_cols) for j in range(pieces)]
    count = len(units)
    tile = 16
    step = shard // (5 * tile) * tile
    direct = shard - step
    middle = shard // 2
    first = middle // tile // 2 * tile
    second = middle - first

    def view(unit, block, start, size):
        _, whole, column, columns = units[unit]
        begin = pl.multiple_of(block * shard + start, tile)
        return whole.at[pl.ds(begin, size), pl.ds(column, columns)]

    def own_view(unit, start, size):
        source, _, column, columns = units[unit]
        return source.at[pl.ds(pl.multiple_of(start, tile), size), pl.ds(column, columns)]

    def remote(unit, which, source, target, device):
        return pltpu.make_async_remote_copy(
            src_ref=source,
            dst_ref=target,
            send_sem=send_sem.at[unit, which],
            recv_sem=recv_sem.at[unit, which],
            device_id=device,
            device_id_type=MESH,
        )

    def moved(unit, which, block, start, size, device):
        span = view(unit, block, start, size)
        return remote(unit, which, span, span, device)

    def split(unit):
        return (second, first) if unit % 2 else (first, second)

    copies = []
    locals_ = []
    for u in range(count):
        via_y, via_z = split(u)
        d0 = lane * step
        m0 = lane * middle
        copies.append([
            remote(u, 0, own_view(u, d0, direct), view(u, own, d0, direct), y_dev),
            remote(u, 1, own_view(u, d0, direct), view(u, own, d0, direct), z_dev),
            remote(u, 2, own_view(u, 0, shard), view(u, own, 0, shard), core_dev),
            moved(u, 3, from_y, lane * direct, step, x_dev),
            moved(u, 4, from_y, m0 + via_y, via_z, z_dev),
            moved(u, 5, from_y, 0, shard, core_dev),
            moved(u, 6, from_z, lane * direct, step, x_dev),
            moved(u, 7, from_z, m0, via_y, y_dev),
            moved(u, 8, from_z, 0, shard, core_dev),
            moved(u, 9, from_yz, m0 + via_y, via_z, x_dev),
            moved(u, 10, from_yz, m0, via_y, x_dev),
            moved(u, 11, from_yz, 0, shard, core_dev),
        ])
        locals_.append(
            pltpu.make_async_copy(own_view(u, 0, shard), view(u, own, 0, shard), local_sem.at[u])
        )

    def begin(u):
        if u < count:
            copies[u][0].start()
            copies[u][1].start()
            copies[u][2].start()
            locals_[u].start()

    def arrive(u):
        c = copies[u]
        c[0].wait_recv()
        c[3].start()
        c[4].start()
        c[1].wait_recv()
        c[6].start()
        c[7].start()

    def relay(u):
        c = copies[u]
        c[4].wait_recv()
        c[9].start()
        c[7].wait_recv()
        c[10].start()
        c[3].wait_recv()
        c[5].start()
        c[6].wait_recv()
        c[8].start()

    def last(u):
        c = copies[u]
        c[9].wait_recv()
        c[10].wait_recv()
        c[11].start()

    def complete(u):
        c = copies[u]
        for k in (2, 5, 8, 11):
            c[k].wait_recv()
        locals_[u].wait()

    def advance(t):
        if 0 <= t - 2 < count:
            last(t - 2)
        if 0 <= t - 1 < count:
            relay(t - 1)
        if t < count:
            arrive(t)
            begin(t + 2)

    begin(0)
    begin(1)
    for load in loads:
        load.wait()

    def row_of(ref):
        return ref[...].reshape(1, ref.shape[0]).astype(F32)

    b_row[...] = row_of(b_proj_ref)
    place = lax.broadcasted_iota(jnp.int32, (rows, rows), 0)
    column = lax.broadcasted_iota(jnp.int32, (rows, rows), 1)
    order = (column == 2 * (place % half) + place // half).astype(BF16)
    frames = jnp.dot(order, frames_ref[...], preferred_element_type=F32)
    residual[...] = frames
    normed_in[...] = norm_rows(
        frames, row_of(gain1_ref), row_of(bias1_ref)
    ).astype(BF16)
    row_window = jnp.zeros((rows, rows), jnp.int32)
    column_window = jnp.zeros((rows, rows), jnp.int32)
    end = jnp.int32(0)
    for j in range(pairs_ref.shape[1]):
        end = end + pairs_ref[0, j]
        row_window += (place % half >= end).astype(jnp.int32)
        column_window += (column % half >= end).astype(jnp.int32)
    mask[...] = jnp.where(row_window == column_window, 0.0, -1e30).astype(F32)

    block = 256

    def project(unit):
        @pl.loop(0, width // block)
        def _(i):
            cols = pl.ds(pl.multiple_of(unit * width + i * block, block), block)
            qkv[:, cols] = jnp.dot(
                normed_in[...], whole_qkv[:, cols], preferred_element_type=F32
            ).astype(BF16)

    pair = 2 * HEAD
    upper = lax.broadcasted_iota(jnp.int32, (rows, pair), 1) >= HEAD

    def softmax(scores):
        scores = scores * HEAD ** (-0.5) + mask[...]
        powers = jnp.exp(scores - jnp.max(scores, axis=1, keepdims=True))
        return (powers * (1.0 / jnp.sum(powers, axis=1, keepdims=True))).astype(BF16)

    def heads(low, high):
        @pl.loop(low, high)
        def _(i):
            at = pl.multiple_of(i * pair, pair)
            queries = qkv[:, pl.ds(at, pair)]
            keys = qkv[:, pl.ds(pl.multiple_of(width + at, pair), pair)]
            values = qkv[:, pl.ds(pl.multiple_of(2 * width + at, pair), pair)]
            results = []
            for part in (0, 1):
                chosen = jnp.where(upper == (part == 1), queries, jnp.zeros_like(queries))
                scores = lax.dot_general(
                    chosen, keys, (((1,), (1,)), ((), ())), preferred_element_type=F32
                )
                results.append(jnp.dot(softmax(scores), values, preferred_element_type=F32))
            attended[:, pl.ds(at, pair)] = jnp.where(upper, results[1], results[0]).astype(BF16)

    total = width // pair
    advance(0)
    advance(1)
    advance(2)
    complete(0)
    project(0)
    advance(3)
    complete(1)
    project(1)
    advance(4)
    complete(2)
    project(2)
    heads(0, total // 2)
    advance(5)
    heads(total // 2, total)
    advance(6)
    complete(3)

    @pl.loop(0, width // block)
    def _(i):
        cols = pl.ds(pl.multiple_of(i * block, block), block)
        residual[:, cols] += jnp.dot(
            attended[...], whole_out[:, cols], preferred_element_type=F32
        )

    pooled = (residual[0:half, :] + residual[half:rows, :]) * 0.5
    normed = norm_rows(pooled, row_of(gain2_ref), row_of(bias2_ref)).astype(BF16)
    capacity = 2 * half // devices
    stride = buffer.shape[0] // devices
    across = lax.broadcasted_iota(jnp.int32, (half, half), 1)
    down = lax.broadcasted_iota(jnp.int32, (half, half), 0)
    dest = route_ref[pl.ds(r, 1), :].astype(F32)
    dest_down = jnp.sum(jnp.where(across == down, dest, 0.0), axis=1, keepdims=True)
    earlier = jnp.where((dest_down == dest) & (down < across), 1.0, 0.0)
    target = dest * stride + jnp.sum(earlier, axis=0, keepdims=True)
    slot = lax.broadcasted_iota(jnp.int32, (buffer.shape[0], half), 0)
    picker = (slot == target.astype(jnp.int32)).astype(BF16)
    buffer[...] = jnp.dot(picker, normed, preferred_element_type=F32).astype(BF16)

    def exchange(i):
        to = (r + i) % devices
        return pltpu.make_async_remote_copy(
            src_ref=buffer.at[pl.ds(pl.multiple_of(to * stride, tile), stride), :],
            dst_ref=arrived.at[pl.ds(pl.multiple_of(r * stride, tile), stride), :],
            send_sem=rows_send.at[i],
            recv_sem=rows_recv.at[i],
            device_id=(g, to),
            device_id_type=MESH,
        )

    @pl.loop(1, devices)
    def _(i):
        exchange(i).start()

    mine_rows = pl.ds(pl.multiple_of(r * stride, tile), stride)
    stay = pltpu.make_async_copy(
        buffer.at[mine_rows, :], arrived.at[mine_rows, :], local_sem.at[count]
    )
    stay.start()
    advance(7)
    advance(8)

    @pl.loop(1, devices)
    def _(i):
        exchange(i).wait_recv()

    stay.wait()
    slots = devices * capacity
    if capacity == stride:
        packed[...] = arrived[...]
    else:
        row = lax.broadcasted_iota(jnp.int32, (slots, devices * stride), 0)
        wide = lax.broadcasted_iota(jnp.int32, (slots, devices * stride), 1)
        keep = (wide == row // capacity * stride + row % capacity).astype(BF16)
        packed[...] = jnp.dot(keep, arrived[...], preferred_element_type=F32).astype(BF16)
    sender = lax.broadcasted_iota(jnp.int32, (slots, devices), 1)
    place = lax.broadcasted_iota(jnp.int32, (slots, devices), 0)
    spread = (place // capacity == sender).astype(BF16)
    named = jnp.where(route_ref[...] == r, 1.0, 0.0).astype(BF16)
    filled = jnp.sum(
        jnp.dot(spread, named, preferred_element_type=F32), axis=1, keepdims=True
    )
    order = lax.broadcasted_iota(jnp.int32, (slots, 1), 0) % capacity
    valid = order.astype(F32) < filled

    def embed(piece):
        @pl.loop(0, proj_cols // block)
        def _(i):
            cols = pl.ds(pl.multiple_of(piece * proj_cols + i * block, block), block)
            product = jnp.dot(packed[...], whole_proj[:, cols], preferred_element_type=F32)
            embed_ref[:, cols] = jnp.where(valid, product + b_row[:, cols], 0.0).astype(BF16)

    complete(4)
    embed(0)
    complete(5)
    embed(1)
    advance(9)
    complete(6)
    embed(2)
    complete(7)
    embed(3)
    for u in range(count):
        for k in range(12):
            copies[u][k].wait_send()

    @pl.loop(1, devices)
    def _(i):
        exchange(i).wait_send()


def rms_kernel(audio_ref, text_ref, gain_ref, out_ref):
    j = pl.program_id(0)
    steps = pl.num_programs(0) // 2

    def write(ref):
        values = ref[...].astype(F32)
        gain = gain_ref[...].reshape(1, gain_ref.shape[0]).astype(F32)
        mean = jnp.mean(values * values, axis=1, keepdims=True)
        out_ref[...] = (values * lax.rsqrt(mean + 1e-06) * gain).astype(BF16)

    @pl.when(j < steps)
    def _():
        write(audio_ref)

    @pl.when(j >= steps)
    def _():
        write(text_ref)


def body(
    frames, ln1_gain, ln1_bias, w_qkv, w_out, ln2_gain, ln2_bias, w_proj, b_proj,
    text_embed, rms_gain, window_pairs, row_route,
):
    rows, width = frames.shape
    devices = lax.axis_size("req")
    pooled_rows = rows // 2
    capacity = 2 * pooled_rows // devices
    slots = devices * capacity
    out_width = w_proj.shape[1]
    full = GROUP * w_qkv.shape[0]
    vmem = pl.BlockSpec(memory_space=pltpu.VMEM)
    hbm = pl.BlockSpec(memory_space=pl.ANY)
    units = 8
    stride = max(capacity, 16)
    route_table = row_route.reshape(devices, pooled_rows)
    embed = pl.pallas_call(
        encoder_kernel,
        out_shape=jax.ShapeDtypeStruct((slots, out_width), BF16),
        in_specs=[hbm] * 7 + [vmem] + [hbm] * 3,
        out_specs=vmem,
        scratch_shapes=[
            pltpu.VMEM((full, 3 * width), BF16),
            pltpu.VMEM((full, width), BF16),
            pltpu.VMEM((full, out_width), BF16),
            pltpu.VMEM((rows, width), BF16),
            pltpu.VMEM((width,), BF16),
            pltpu.VMEM((width,), BF16),
            pltpu.VMEM((width,), BF16),
            pltpu.VMEM((width,), BF16),
            pltpu.VMEM((out_width,), BF16),
            pltpu.VMEM((1, out_width), F32),
            pltpu.SMEM(window_pairs.shape, jnp.int32),
            pltpu.VMEM((rows, width), BF16),
            pltpu.VMEM((rows, width), F32),
            pltpu.VMEM((rows, 3 * width), BF16),
            pltpu.VMEM((rows, width), BF16),
            pltpu.VMEM((rows, rows), F32),
            pltpu.VMEM((devices * stride, width), BF16),
            pltpu.VMEM((devices * stride, width), BF16),
            pltpu.VMEM((slots, width), BF16),
            pltpu.SemaphoreType.DMA((units, 12)),
            pltpu.SemaphoreType.DMA((units, 12)),
            pltpu.SemaphoreType.DMA((units + 1,)),
            pltpu.SemaphoreType.DMA((7,)),
            pltpu.SemaphoreType.DMA((devices,)),
            pltpu.SemaphoreType.DMA((devices,)),
        ],
        compiler_params=pltpu.CompilerParams(
            collective_id=0, has_side_effects=True, vmem_limit_bytes=58 * 2**20
        ),
        name="encoder",
    )(
        frames, ln1_gain, ln1_bias, ln2_gain, ln2_bias, b_proj, window_pairs, route_table,
        w_qkv, w_out, w_proj,
    )
    text_rows = text_embed.shape[0]
    steps = 2
    audio_block = slots // steps
    return pl.pallas_call(
        rms_kernel,
        grid=(2 * steps,),
        out_shape=jax.ShapeDtypeStruct((slots + text_rows, out_width), BF16),
        in_specs=[
            pl.BlockSpec((audio_block, out_width), lambda j: (jnp.minimum(j, steps - 1), 0)),
            pl.BlockSpec((audio_block, out_width), lambda j: (jnp.maximum(j - steps, 0), 0)),
            pl.BlockSpec((out_width,), lambda j: (0,)),
        ],
        out_specs=pl.BlockSpec((audio_block, out_width), lambda j: (j, 0)),
        compiler_params=pltpu.CompilerParams(vmem_limit_bytes=58 * 2**20),
        name="rms",
    )(embed, text_embed, rms_gain)


def solution(mesh):
    in_specs = (
        P(("groups", "req"), None),
        P(),
        P(),
        P("req", None),
        P("req", None),
        P(),
        P(),
        P("req", None),
        P(),
        P(("groups", "req"), None),
        P(),
        P(("groups", "req"), None),
        P("groups", None),
    )
    out_specs = P(("groups", "req"), None)
    return jax.shard_map(body, mesh=mesh, in_specs=in_specs, out_specs=out_specs, check_vma=False)
```
